32 devices in a mesh: groups: 2 (over x), fsdp: 4 (over y, core), tp: 4 (over z).
Axes of the slice: x: 2, y: 2, z: 4, core: 2. Of those that a mesh axis runs over, the one named last changes fastest.
Arguments:
- layer_inputs: bfloat16 [4, 768, 4608], P(None, ('groups', 'fsdp'), 'tp'), parts along dimension 1, may hold values from -6 to 6
- norm_gain: bfloat16 [4608], replicated, may hold values from 0.099609375 to 1.8984375
- query_weight: bfloat16 [4608, 2048], P(None, 'tp'), may hold values from -0.75 to 0.75
- key_weight: bfloat16 [4608, 1024], P(None, 'tp'), may hold values from -0.09375 to 0.09375
- value_weight: bfloat16 [4608, 1024], P(None, 'tp'), may hold values from -0.09375 to 0.09375
- output_weight: bfloat16 [2048, 4608], P('tp'), may hold values from -0.5 to 0.5
- query_down: bfloat16 [9216, 64], P(('groups', 'fsdp')), parts along dimension 0, may hold values from -0.75 to 0.75
- key_down: bfloat16 [9216, 64], P(('groups', 'fsdp')), parts along dimension 0, may hold values from -0.09375 to 0.09375
- value_down: bfloat16 [9216, 64], P(('groups', 'fsdp')), parts along dimension 0, may hold values from -0.09375 to 0.09375
- output_down: bfloat16 [4096, 64], P(('groups', 'fsdp')), parts along dimension 0, may hold values from -0.125 to 0.125
- query_up: bfloat16 [4096, 64], P(('groups', 'fsdp')), parts along dimension 0, may hold values from -0.375 to 0.375
- key_up_factor: bfloat16 [2048, 64], P(('groups', 'fsdp')), parts along dimension 0, may hold values from -0.375 to 0.375
- value_up: bfloat16 [2048, 64], P(('groups', 'fsdp')), parts along dimension 0, may hold values from -0.375 to 0.375
- output_up: bfloat16 [9216, 64], P(('groups', 'fsdp')), parts along dimension 0, may hold values from -0.375 to 0.375
- cached_keys: bfloat16 [768, 8, 96, 128], P(('groups', 'fsdp'), 'tp'), parts along dimension 0, may hold values from -9 to 9
- cached_values: bfloat16 [768, 8, 96, 128], P(('groups', 'fsdp'), 'tp'), parts along dimension 0, may hold values from -6 to 6
- context_lengths: int32 [768], P(('groups', 'fsdp')), parts along dimension 0, may hold values from 1 to 96, as said below
Outputs:
- attention_out: bfloat16 [4, 768, 4608], P(None, ('groups', 'fsdp'), 'tp'), parts along dimension 1
The draws below stay inside these ranges and needn't reach their ends.
There are 2 independent parts, one for each index of `groups`. The reference program is written for one: setup_inputs(seed, part) draws one part's arguments, and reference() takes and returns one part's arrays. A program takes and returns all parts, laid end to end along the dimension named above; an argument that names none is the same for every part. Nothing has to cross between parts.
Inputs may be any that keep to these rules, and one draw needn't show every extreme that they name: `context_lengths`: in each aligned block of 96 rows, at least one row has all 96 slots live.
All inputs are finite; a program needn't handle non-finite values.
Results may differ from the reference program's by a relative error of at most 0.012.
The reference program's roundings to bfloat16 on the way count: a program that leaves them out, or rounds other values in their place, can miss the bound.
Values may be sent and summed in bfloat16 or wider, within the bound.
A program may use at most 128 MiB of HBM per device.

```python
import jax
import jax.numpy as jnp
from jax import lax

D = 4608
HEADS = 16
KV_HEADS = 8
HEAD_FEATURES = 128
RANK = 64
STEPS = 4
ROWS_DEV = 96
CTX = 96
ROWS = 384
Q_WIDTH = 2048
KV_WIDTH = 1024


def draw_context_lengths(key, part):
    key = jax.random.fold_in(key, 11)
    first_key, second_key = jax.random.split(key)
    drawn = jax.random.randint(first_key, (ROWS,), 1, CTX + 1)
    chosen = jax.random.randint(second_key, (ROWS // ROWS_DEV,), 0, ROWS_DEV)
    row_ids = jnp.arange(ROWS)
    filled = row_ids % ROWS_DEV == chosen[row_ids // ROWS_DEV]
    return jnp.where(filled, CTX, drawn).astype(jnp.int32)


def shard_levels(stream_key, extent, shards, low, largest):
    factor_of = 1.0
    for dim, blocks in shards:
        draws = jax.random.uniform(jax.random.fold_in(jax.random.fold_in(stream_key, 6), dim), (blocks,), jnp.float32, low / len(shards), largest / len(shards))
        factor_of = factor_of * jnp.repeat(jnp.exp(draws), extent[dim] // blocks).reshape((-1,) + (1,) * (len(extent) - 1 - dim))
    return factor_of


def bell_draw(own_key, shape, spread, most, pieces=(), kind=jnp.bfloat16):
    factor_of = shard_levels(own_key, shape, pieces, -0.22, 0.18) if pieces else 1.0
    result = jax.random.normal(own_key, shape, jnp.float32) * spread * factor_of
    return jnp.minimum(jnp.maximum(result, -most), most).astype(kind)


def setup_inputs(seed: int = 0, part: int = 0) -> dict:
    key_list = jax.random.split(jax.random.key(seed), 18)
    own_keys = jax.random.split(jax.random.fold_in(key_list[17], part), 18)
    return {
        "layer_inputs": bell_draw(own_keys[0], (STEPS, ROWS, D), 1.0, 6.0, ((1, 4), (2, 4))),
        "norm_gain": jnp.clip(1.0 + 0.18 * jax.random.normal(key_list[1], (D,), jnp.float32), 0.099609375, 1.8984375).astype(jnp.bfloat16),
        "query_weight": bell_draw(key_list[2], (D, Q_WIDTH), (D // 64) ** -0.5, 0.75, ((1, 4),)),
        "key_weight": bell_draw(key_list[3], (D, KV_WIDTH), D ** -0.5, 0.09375, ((1, 4),)),
        "value_weight": bell_draw(key_list[4], (D, KV_WIDTH), D ** -0.5, 0.09375, ((1, 4),)),
        "output_weight": bell_draw(key_list[5], (Q_WIDTH, D), HEAD_FEATURES ** -0.5, 0.5, ((0, 4),)),
        "query_down": bell_draw(own_keys[6], (D, RANK), (D // 64) ** -0.5, 0.75, ((0, 4),)),
        "key_down": bell_draw(own_keys[7], (D, RANK), D ** -0.5, 0.09375, ((0, 4),)),
        "value_down": bell_draw(own_keys[8], (D, RANK), D ** -0.5, 0.09375, ((0, 4),)),
        "output_down": bell_draw(own_keys[9], (Q_WIDTH, RANK), Q_WIDTH ** -0.5, 0.125, ((0, 4),)),
        "query_up": bell_draw(own_keys[10], (Q_WIDTH, RANK), (4 * RANK) ** -0.5, 0.375, ((0, 4),)),
        "key_up_factor": bell_draw(own_keys[11], (KV_WIDTH, RANK), (4 * RANK) ** -0.5, 0.375, ((0, 4),)),
        "value_up": bell_draw(own_keys[12], (KV_WIDTH, RANK), (4 * RANK) ** -0.5, 0.375, ((0, 4),)),
        "output_up": bell_draw(own_keys[13], (D, RANK), (4 * RANK) ** -0.5, 0.375, ((0, 4),)),
        "cached_keys": bell_draw(own_keys[14], (ROWS, KV_HEADS, CTX, HEAD_FEATURES), 1.5, 9.0, ((0, 4), (1, 4))),
        "cached_values": bell_draw(own_keys[15], (ROWS, KV_HEADS, CTX, HEAD_FEATURES), 1.0, 6.0, ((0, 4), (1, 4))),
        "context_lengths": draw_context_lengths(jax.random.fold_in(jax.random.fold_in(key_list[17], part), 71), part),
    }


ADAPTER_SCALE = 2.0
SOFTCAP = 50.0
QUERY_SCALE = 144.0 ** (-0.5)
RMS_EPS = 1e-06
ROPE_BASE = 10000.0

def merged(base_weight, down, up):
    weight_update = jnp.dot(down, up.T, preferred_element_type=jnp.float32)
    return (base_weight.astype(jnp.float32) + ADAPTER_SCALE * weight_update).astype(jnp.bfloat16)

def rotate(values, position):
    half = values.shape[-1] // 2
    freq = ROPE_BASE ** (-2.0 * jnp.arange(half, dtype=jnp.float32) / values.shape[-1])
    angle = position[..., None] * freq
    cosine = jnp.cos(angle)
    sine = jnp.sin(angle)
    first = values[..., :half]
    second = values[..., half:]
    return jnp.concatenate([first * cosine - second * sine, second * cosine + first * sine], axis=-1)

def normalize(inputs, gain):
    wide = inputs.astype(jnp.float32)
    factor = lax.rsqrt(lax.optimization_barrier(jnp.mean(wide * wide, axis=-1, keepdims=True)) + RMS_EPS)
    return (wide * factor * gain.astype(jnp.float32)).astype(jnp.bfloat16)

def reference(layer_inputs, norm_gain, query_weight, key_weight, value_weight, output_weight, query_down, key_down, value_down, output_down, query_up, key_up_factor, value_up, output_up, cached_keys, cached_values, context_lengths):
    query_matrix = merged(query_weight, query_down, query_up)
    w_key = merged(key_weight, key_down, key_up_factor)
    w_value = merged(value_weight, value_down, value_up)
    w_output = merged(output_weight, output_down, output_up)
    nrows = layer_inputs.shape[1]
    per_group = HEADS // KV_HEADS
    keys_wide = cached_keys.astype(jnp.float32)
    values_wide = cached_values.astype(jnp.float32)
    new_keys = jnp.zeros((nrows, KV_HEADS, STEPS, HEAD_FEATURES), jnp.bfloat16)
    new_values = jnp.zeros((nrows, KV_HEADS, STEPS, HEAD_FEATURES), jnp.bfloat16)
    slots = jnp.arange(CTX, dtype=jnp.int32)
    marks = jnp.arange(STEPS, dtype=jnp.int32)
    mask_old = (slots[None, :] < context_lengths[:, None])[:, None, None, :]
    results = []
    for step_index in range(STEPS):
        normed = normalize(layer_inputs[step_index], norm_gain)
        query = jnp.dot(normed, query_matrix, preferred_element_type=jnp.float32).reshape(nrows, KV_HEADS, per_group, HEAD_FEATURES)
        key_now = jnp.dot(normed, w_key, preferred_element_type=jnp.float32).reshape(nrows, KV_HEADS, HEAD_FEATURES)
        value_now = jnp.dot(normed, w_value, preferred_element_type=jnp.float32).reshape(nrows, KV_HEADS, HEAD_FEATURES)
        position = (context_lengths + step_index).astype(jnp.float32)
        query_rot = (rotate(query, position[:, None, None]) * QUERY_SCALE).astype(jnp.bfloat16)
        key_rot = rotate(key_now, position[:, None]).astype(jnp.bfloat16)
        new_keys = new_keys.at[:, :, step_index].set(key_rot)
        new_values = new_values.at[:, :, step_index].set(value_now.astype(jnp.bfloat16))
        query_wide = query_rot.astype(jnp.float32)
        score_old = jnp.einsum('rgpd,rgcd->rgpc', query_wide, keys_wide)
        score_new = jnp.einsum('rgpd,rgsd->rgps', query_wide, new_keys.astype(jnp.float32))
        mask_new = (marks <= step_index)[None, None, None, :]
        expo_old = jnp.where(mask_old, jnp.exp(SOFTCAP * jnp.tanh(score_old / SOFTCAP)), 0.0)
        expo_new = jnp.where(mask_new, jnp.exp(SOFTCAP * jnp.tanh(score_new / SOFTCAP)), 0.0)
        total = lax.optimization_barrier(jnp.sum(expo_old, axis=-1, keepdims=True)) + lax.optimization_barrier(jnp.sum(expo_new, axis=-1, keepdims=True))
        weight_old = (expo_old / total).astype(jnp.bfloat16).astype(jnp.float32)
        weight_new = (expo_new / total).astype(jnp.bfloat16).astype(jnp.float32)
        attended = jnp.einsum('rgpc,rgcd->rgpd', weight_old, values_wide) + jnp.einsum('rgps,rgsd->rgpd', weight_new, new_values.astype(jnp.float32))
        attended = attended.astype(jnp.bfloat16).reshape(nrows, HEADS * HEAD_FEATURES)
        results.append(jnp.dot(attended, w_output, preferred_element_type=jnp.float32).astype(jnp.bfloat16))
    return jnp.stack(results)
```

```python
import functools

import jax
import jax.numpy as jnp
from jax import lax
from jax.experimental import pallas as pl
from jax.experimental.pallas import tpu as pltpu
from jax.sharding import PartitionSpec as P

HEADS = 16
KV_HEADS = 8
HF = 128
STEPS = 4
CHUNK = 32

ADAPTER_SCALE = 2.0
SOFTCAP = 50.0
QUERY_SCALE = 144.0 ** (-0.5)
RMS_EPS = 1e-06
ROPE_BASE = 10000.0


def merged(base_weight, down, up):
    weight_update = jnp.dot(down, up.T, preferred_element_type=jnp.float32)
    return (base_weight.astype(jnp.float32) + ADAPTER_SCALE * weight_update).astype(jnp.bfloat16)


def rope_tables(context_lengths):
    half = HF // 2
    freq = ROPE_BASE ** (-2.0 * jnp.arange(half, dtype=jnp.float32) / HF)
    steps = jnp.arange(STEPS, dtype=jnp.int32)
    position = (context_lengths[None, :] + steps[:, None]).astype(jnp.float32)
    angle = position[..., None] * freq
    cosine = jnp.cos(angle)
    sine = jnp.sin(angle)
    return (
        jnp.concatenate([cosine, cosine], axis=-1),
        jnp.concatenate([-sine, sine], axis=-1),
    )


def attend_chunk(kv_local, load, cos, sin, lens, ck_ref, cv_ref, store, q3, k3, v3, a3):
    per = HEADS // KV_HEADS
    for s in range(STEPS):
        c, n = cos(s), sin(s)

        def rot(u):
            return u * c + pltpu.roll(u, HF // 2, 1) * n

        for g in range(kv_local):
            for p in range(per):
                u = rot(load(0, s, g * per + p)) * QUERY_SCALE
                q3[:, g * 8 + s * per + p, :] = u
            k3[:, g * 8 + s, :] = rot(load(1, s, g))
            v3[:, g * 8 + s, :] = load(2, s, g)

    slot = lax.broadcasted_iota(jnp.int32, (8, HF), 1)
    step_of = lax.broadcasted_iota(jnp.int32, (8, HF), 0) // per
    ctx = ck_ref.shape[2]
    new_live = (slot >= ctx) & (slot <= ctx + step_of)
    pad = jnp.zeros((HF - ctx - 8, HF), jnp.float32)
    group = 4

    def body(i, carry):
        for j in range(group):
            r = i * group + j
            live = new_live | (slot < lens(r))
            for g in range(kv_local):
                q = q3[r, pl.ds(g * 8, 8), :].astype(jnp.bfloat16)
                kn = jnp.concatenate([k3[r, pl.ds(g * 8, 8), :], pad]).astype(jnp.bfloat16)
                vn = jnp.concatenate([v3[r, pl.ds(g * 8, 8), :], pad]).astype(jnp.bfloat16)
                keys = jnp.concatenate([ck_ref[r, g], kn])
                values = jnp.concatenate([cv_ref[r, g], vn])
                score = lax.dot_general(
                    q, keys, (((1,), (1,)), ((), ())), preferred_element_type=jnp.float32
                )
                expo = jnp.where(live, jnp.exp(SOFTCAP * jnp.tanh(score / SOFTCAP)), 0.0)
                total = jnp.sum(expo, axis=-1, keepdims=True)
                weight = (expo / total).astype(jnp.bfloat16)
                a3[r, pl.ds(g * 8, 8), :] = jnp.dot(
                    weight, values, preferred_element_type=jnp.float32
                )
        return carry

    lax.fori_loop(0, CHUNK // group, body, 0)
    for s in range(STEPS):
        for g in range(kv_local):
            for p in range(per):
                store(s, g * per + p, a3[:, g * 8 + s * per + p, :].astype(jnp.bfloat16))


def attention_kernel(kv_local, lens_ref, q_ref, k_ref, v_ref, cos_ref, sin_ref, ck_ref, cv_ref, o_ref, q3, k3, v3, a3):
    k3[...] = jnp.zeros_like(k3)
    v3[...] = jnp.zeros_like(v3)
    base = pl.program_id(0) * CHUNK
    refs = (q_ref, k_ref, v_ref)

    def load(which, s, h):
        return refs[which][s, :, pl.ds(h * HF, HF)]

    def store(s, h, value):
        o_ref[s, :, pl.ds(h * HF, HF)] = value

    attend_chunk(
        kv_local, load, lambda s: cos_ref[s], lambda s: sin_ref[s],
        lambda r: lens_ref[base + r], ck_ref, cv_ref, store, q3, k3, v3, a3,
    )


def attention(lens, q, k, v, cos, sin, ck, cv):
    rows = lens.shape[0]
    kv_local = ck.shape[1]
    ql, kl = q.shape[-1], k.shape[-1]
    tok = lambda w: pl.BlockSpec((STEPS, CHUNK, w), lambda i, *_: (0, i, 0))
    cache = pl.BlockSpec((CHUNK,) + ck.shape[1:], lambda i, *_: (i, 0, 0, 0))
    scratch = pltpu.VMEM((CHUNK, kv_local * 8, HF), jnp.float32)
    return pl.pallas_call(
        functools.partial(attention_kernel, kv_local),
        out_shape=jax.ShapeDtypeStruct((STEPS, rows, ql), jnp.bfloat16),
        grid_spec=pltpu.PrefetchScalarGridSpec(
            num_scalar_prefetch=1,
            grid=(rows // CHUNK,),
            in_specs=[tok(ql), tok(kl), tok(kl), tok(HF), tok(HF), cache, cache],
            out_specs=tok(ql),
            scratch_shapes=[scratch] * 4,
        ),
        compiler_params=pltpu.CompilerParams(vmem_limit_bytes=40 * 2**20),
    )(lens, q, k, v, cos, sin, ck, cv)


def shards(
    x, norm_gain, query_weight, key_weight, value_weight, output_weight,
    query_down, key_down, value_down, output_down,
    query_up, key_up_factor, value_up, output_up,
    cached_keys, cached_values, context_lengths,
):
    tp_rank = lax.axis_index("tp")
    n_fsdp = lax.axis_size("fsdp")
    nrows = x.shape[1]
    ql, kl = query_weight.shape[1], key_weight.shape[1]
    sizes = [query_down.shape[0], value_down.shape[0], output_down.shape[0], key_up_factor.shape[0]]
    pack = jnp.concatenate([
        jnp.concatenate([query_down, key_down], 1),
        jnp.concatenate([value_down, output_up], 1),
        jnp.concatenate([output_down, query_up], 1),
        jnp.concatenate([key_up_factor, value_up], 1),
    ])
    every = lax.all_gather(pack, "fsdp", axis=0)
    xs = lax.all_gather(x, "tp", axis=2, tiled=True)
    rank = query_down.shape[1]
    ends = [0]
    for size in sizes:
        ends.append(ends[-1] + size)
    parts = [every[:, a:b].reshape(-1, 2 * rank) for a, b in zip(ends[:-1], ends[1:])]

    def block(whole, width):
        return lax.dynamic_slice_in_dim(whole, tp_rank * width, width, 0)

    third = block(parts[2], ql)
    fourth = block(parts[3], kl)
    w_query = merged(query_weight, parts[0][:, :rank], third[:, rank:])
    w_key = merged(key_weight, parts[0][:, rank:], fourth[:, :rank])
    w_value = merged(value_weight, parts[1][:, :rank], fourth[:, rank:])
    w_output = merged(output_weight, third[:, :rank], parts[1][:, rank:])
    wide = xs.astype(jnp.float32)
    factor = lax.rsqrt(jnp.mean(wide * wide, axis=-1, keepdims=True) + RMS_EPS)
    normed = (wide * factor * norm_gain.astype(jnp.float32)).astype(jnp.bfloat16)
    q = jnp.dot(normed, w_query, preferred_element_type=jnp.float32)
    k = jnp.dot(normed, w_key, preferred_element_type=jnp.float32)
    v = jnp.dot(normed, w_value, preferred_element_type=jnp.float32)
    cos, sin = rope_tables(context_lengths)
    attended = attention(context_lengths, q, k, v, cos, sin, cached_keys, cached_values)
    terms = jnp.dot(attended, w_output, preferred_element_type=jnp.float32)
    return lax.psum_scatter(terms.astype(jnp.bfloat16), "tp", scatter_dimension=2, tiled=True)


def solution(mesh):
    fs = ("groups", "fsdp")
    return jax.shard_map(
        shards,
        mesh=mesh,
        in_specs=(
            P(None, fs, "tp"), P(),
            P(None, "tp"), P(None, "tp"), P(None, "tp"), P("tp", None),
            P(fs, None), P(fs, None), P(fs, None), P(fs, None),
            P(fs, None), P(fs, None), P(fs, None), P(fs, None),
            P(fs, "tp", None, None), P(fs, "tp", None, None), P(fs),
        ),
        out_specs=P(None, fs, "tp"),
        check_vma=False,
    )
```

```python
import functools

import jax
import jax.numpy as jnp
from jax import lax
from jax.experimental import pallas as pl
from jax.experimental.pallas import tpu as pltpu
from jax.sharding import PartitionSpec as P

HEADS = 16
KV_HEADS = 8
HF = 128
STEPS = 4
CHUNK = 32

ADAPTER_SCALE = 2.0
SOFTCAP = 50.0
QUERY_SCALE = 144.0 ** (-0.5)
RMS_EPS = 1e-06
ROPE_BASE = 10000.0


def rope_tables(context_lengths):
    half = HF // 2
    freq = ROPE_BASE ** (-2.0 * jnp.arange(half, dtype=jnp.float32) / HF)
    steps = jnp.arange(STEPS, dtype=jnp.int32)
    position = (context_lengths[None, :] + steps[:, None]).astype(jnp.float32)
    angle = position[..., None] * freq
    cosine = jnp.cos(angle)
    sine = jnp.sin(angle)
    return (
        jnp.concatenate([cosine, cosine], axis=-1),
        jnp.concatenate([-sine, sine], axis=-1),
    )


MESH = pl.DeviceIdType.MESH
TOK = STEPS * CHUNK
NT = (((1,), (1,)), ((), ()))


def attend(kv_local, qkv, cos, sin, length, ckb, cvb, base, at, q3, k3, v3, a3):
    per = HEADS // KV_HEADS
    ql, kl = kv_local * per * HF, kv_local * HF
    for s in range(STEPS):
        c, n = cos(s), sin(s)
        rows = pl.ds(s * CHUNK, CHUNK)

        def rot(u):
            return u * c + pltpu.roll(u, HF // 2, 1) * n

        for g in range(kv_local):
            for p in range(per):
                u = qkv[rows, pl.ds((g * per + p) * HF, HF)]
                q3[:, g * 8 + s * per + p, :] = rot(u) * QUERY_SCALE
            k3[:, g * 8 + s, :] = rot(qkv[rows, pl.ds(ql + g * HF, HF)])
            v3[:, g * 8 + s, :] = qkv[rows, pl.ds(ql + kl + g * HF, HF)]

    slot = lax.broadcasted_iota(jnp.int32, (8, HF), 1)
    step_of = lax.broadcasted_iota(jnp.int32, (8, HF), 0) // per
    ctx = ckb.shape[2]
    new_live = (slot >= ctx) & (slot <= ctx + step_of)
    pad = jnp.zeros((HF - ctx - 8, HF), jnp.float32)
    group = 8

    def step(i, carry):
        pairs = [(i * group + j, g) for j in range(group) for g in range(kv_local)]

        def whole(cache, new, r, g):
            fresh = jnp.concatenate([new[r, pl.ds(g * 8, 8), :], pad]).astype(jnp.bfloat16)
            return jnp.concatenate([cache[base + r, g], fresh])

        scores = jnp.concatenate([
            lax.dot_general(
                q3[r, pl.ds(g * 8, 8), :].astype(jnp.bfloat16), whole(ckb, k3, r, g), NT,
                preferred_element_type=jnp.float32,
            )
            for r, g in pairs
        ])
        live = jnp.concatenate([
            jnp.where(new_live | (slot < length(base + r)), 1.0, 0.0) for r, g in pairs
        ])
        expo = jnp.exp(SOFTCAP * jnp.tanh(scores * (1.0 / SOFTCAP))) * live
        total = jnp.sum(expo, axis=-1, keepdims=True)
        weights = expo / total
        results = [
            jnp.dot(
                weights[8 * j:8 * j + 8].astype(jnp.bfloat16), whole(cvb, v3, r, g),
                preferred_element_type=jnp.float32,
            )
            for j, (r, g) in enumerate(pairs)
        ]
        for (r, g), result in zip(pairs, results):
            a3[r, pl.ds(g * 8, 8), :] = result
        return carry

    lax.fori_loop(0, CHUNK // group, step, 0)
    for s in range(STEPS):
        for g in range(kv_local):
            for p in range(per):
                at[pl.ds(s * CHUNK, CHUNK), pl.ds((g * per + p) * HF, HF)] = a3[
                    :, g * 8 + s * per + p, :
                ].astype(jnp.bfloat16)


def layer_kernel(
    n, n_fsdp, chunks, sizes, wo_split,
    lens, x, gain, wq, wk, wv, wo, pack, cos, sin, ck, cv, out,
    xall, fac, wqkv, wout, ckb, cvb, upqk, upv, odown, normed, qkv, at,
    q3, k3, v3, a3, parts, own, rlo, rhi, outb,
    ag_up, ag_dn, ag_rx, rs_up, rs_dn, rs_lo, rs_hi, fs_y, fs_p, fac_rx,
    x_sem, w_sem, kv_sem, pack_sem, out_sem,
):
    z = lax.axis_index("tp")
    f = lax.axis_index("fsdp")
    ny = n_fsdp // 2
    y, core = f // 2, f % 2
    partner = f + 1 - 2 * core
    m = n_fsdp // n
    s0, s2, s3 = sizes
    ql, kl = wq.shape[1], wk.shape[1]
    width = ql + 2 * kl
    kv_local = kl // HF
    dl = x.shape[2]

    def peer(dy):
        return ((y + dy) % ny) * 2 + core

    local = [
        pltpu.make_async_copy(x.at[:, pl.ds(c * CHUNK, CHUNK), :], xall.at[z, c], x_sem.at[c])
        for c in range(chunks)
    ]
    own_pack = pltpu.make_async_copy(pack, fac.at[f], pack_sem)
    weights = [
        pltpu.make_async_copy(wq, wqkv.at[:, pl.ds(0, ql)], w_sem.at[0]),
        pltpu.make_async_copy(wk, wqkv.at[:, pl.ds(ql, kl)], w_sem.at[1]),
        pltpu.make_async_copy(wv, wqkv.at[:, pl.ds(ql + kl, kl)], w_sem.at[2]),
    ]
    for p in range(n):
        piece = wo.at[p] if wo_split else wo.at[:, pl.ds(p * dl, dl)]
        weights.append(pltpu.make_async_copy(piece, wout.at[p], w_sem.at[3 + p]))
    caches = [
        pltpu.make_async_copy(ck, ckb, kv_sem.at[0]),
        pltpu.make_async_copy(cv, cvb, kv_sem.at[1]),
    ]
    for copy in local + [own_pack] + weights + caches:
        copy.start()

    barrier = pltpu.get_barrier_semaphore()

    def greet(target):
        pl.semaphore_signal(barrier, inc=1, device_id=target, device_id_type=MESH)

    @pl.when(z > 0)
    def _():
        greet({"tp": z - 1})

    @pl.when(z < n - 1)
    def _():
        greet({"tp": z + 1})

    for dy in range(1, ny):
        greet({"fsdp": peer(dy)})
    greet({"fsdp": partner})
    pl.semaphore_wait(barrier, ny + (z + n - 1) // n + (2 * n - 2 - z) // n)

    def ag(o, c, step):
        sem = ag_up if step > 0 else ag_dn
        return pltpu.make_async_remote_copy(
            src_ref=xall.at[o, c], dst_ref=xall.at[o, c], send_sem=sem.at[o, c],
            recv_sem=ag_rx.at[o, c], device_id={"tp": z + step}, device_id_type=MESH,
        )

    def ag_own(c):
        @pl.when(z < n - 1)
        def _():
            ag(z, c, 1).start()

        @pl.when(z > 0)
        def _():
            ag(z, c, -1).start()

    def ag_arrive(c, d):
        @pl.when(z - d >= 0)
        def _():
            ag(z - d, c, 1).wait_recv()

            @pl.when(z < n - 1)
            def _():
                ag(z - d, c, 1).start()

        @pl.when(z + d < n)
        def _():
            ag(z + d, c, -1).wait_recv()

            @pl.when(z > 0)
            def _():
                ag(z + d, c, -1).start()

    def fac_y(dy):
        return pltpu.make_async_remote_copy(
            src_ref=fac.at[f], dst_ref=fac.at[f], send_sem=fs_y.at[dy], recv_sem=fac_rx.at[f],
            device_id={"fsdp": peer(dy)}, device_id_type=MESH,
        )

    def fac_from(slot):
        return pltpu.make_async_remote_copy(
            src_ref=fac.at[slot], dst_ref=fac.at[slot], send_sem=fs_y.at[0],
            recv_sem=fac_rx.at[slot], device_id={"fsdp": partner}, device_id_type=MESH,
        )

    def fac_across(dy):
        slot = peer(dy)
        return pltpu.make_async_remote_copy(
            src_ref=fac.at[slot], dst_ref=fac.at[slot], send_sem=fs_p.at[dy],
            recv_sem=fac_rx.at[slot], device_id={"fsdp": partner}, device_id_type=MESH,
        )

    local[0].wait()
    ag_own(0)
    own_pack.wait()
    for dy in range(1, ny):
        fac_y(dy).start()
    fac_across(0).start()
    local[1].wait()
    ag_own(1)
    for c in range(2, chunks):
        local[c].wait()
    k3[...] = jnp.zeros_like(k3)
    v3[...] = jnp.zeros_like(v3)
    ag_arrive(0, 1)
    for dy in range(1, ny):
        fac_from(peer(dy)).wait_recv()
        fac_across(dy).start()
    for d in range(2, n - 1):
        ag_arrive(0, d)
    for c in range(2, chunks):
        ag_own(c)
    ag_arrive(1, 1)
    for dy in range(ny):
        fac_from(((y + dy) % ny) * 2 + 1 - core).wait_recv()

    def lanes(rows, high):
        lane = lax.broadcasted_iota(jnp.int32, (rows, HF), 1)
        return lane >= HF // 2 if high else lane < HF // 2

    def keep(value, high):
        wide = value.astype(jnp.float32)
        return jnp.where(lanes(value.shape[0], high), wide, 0.0).astype(jnp.bfloat16)

    for i in range(m):
        third = fac[z * m + i, pl.ds(2 * s0, s2), :]
        fourth = fac[z * m + i, pl.ds(2 * s0 + s2, s3), :]
        upqk[pl.ds(i * s2, s2), :] = keep(third, False)
        odown[pl.ds(i * s2, s2), :] = keep(third, True)
        upv[pl.ds(i * s3, s3), :] = keep(fourth, False)
        upqk[pl.ds(ql + i * s3, s3), :] = keep(fourth, True)

    for copy in weights[:3]:
        copy.wait()
    tile = 96
    tiles = s0 // tile

    def merge_in(i, carry):
        shard, t = i // tiles, i % tiles
        first = pl.ds(pl.multiple_of(t * tile, 32), tile)
        second = pl.ds(pl.multiple_of(s0 + t * tile, 32), tile)
        rows = pl.ds(pl.multiple_of(i * tile, 32), tile)
        a = lax.dot_general(fac[shard, first, :], upqk[...], NT, preferred_element_type=jnp.float32)
        b = lax.dot_general(fac[shard, second, :], upv[...], NT, preferred_element_type=jnp.float32)
        left, right = pl.ds(0, ql + kl), pl.ds(ql + kl, kl)
        wqkv[rows, left] = (wqkv[rows, left].astype(jnp.float32) + ADAPTER_SCALE * a).astype(jnp.bfloat16)
        wqkv[rows, right] = (wqkv[rows, right].astype(jnp.float32) + ADAPTER_SCALE * b).astype(jnp.bfloat16)
        return carry

    half = n_fsdp * tiles // 2
    lax.fori_loop(0, half, merge_in, 0)
    for d in range(2, n - 1):
        ag_arrive(1, d)
    lax.fori_loop(half, n_fsdp * tiles, merge_in, 0)
    if chunks > 2:
        ag_arrive(2, 1)
    for copy in weights[3:]:
        copy.wait()
    otile = 64
    otiles = ql // otile

    def merge_out(i, carry):
        p, t = i // otiles, i % otiles
        rows = pl.ds(pl.multiple_of(t * otile, otile), otile)
        up = jnp.concatenate([fac[p * m + j, pl.ds(s0, s0), :] for j in range(m)])
        a = lax.dot_general(odown[rows, :], up, NT, preferred_element_type=jnp.float32)
        wout[p, rows, :] = (wout[p, rows, :].astype(jnp.float32) + ADAPTER_SCALE * a).astype(jnp.bfloat16)
        return carry

    lax.fori_loop(0, n * otiles, merge_out, 0)
    for copy in caches:
        copy.wait()

    def rs(p, c, step):
        return pltpu.make_async_remote_copy(
            src_ref=parts.at[c, p], dst_ref=(rlo if step > 0 else rhi).at[c, p],
            send_sem=(rs_up if step > 0 else rs_dn).at[c, p],
            recv_sem=(rs_lo if step > 0 else rs_hi).at[c, p],
            device_id={"tp": z + step}, device_id_type=MESH,
        )

    def add_in(p, c, landed):
        parts[c, p] = (parts[c, p].astype(jnp.float32) + landed[c, p].astype(jnp.float32)).astype(jnp.bfloat16)

    def rs_first(c):
        @pl.when(z == 0)
        def _():
            for p in range(n - 1, 0, -1):
                rs(p, c, 1).start()

        @pl.when(z == n - 1)
        def _():
            for p in range(n - 1):
                rs(p, c, -1).start()

    def rs_forward(c):
        for k in range(1, n):
            up, dn = n - k, k - 1

            @pl.when((z > 0) & (z < up))
            def _():
                rs(up, c, 1).wait_recv()
                add_in(up, c, rlo)
                rs(up, c, 1).start()

            @pl.when((z < n - 1) & (z > dn))
            def _():
                rs(dn, c, -1).wait_recv()
                add_in(dn, c, rhi)
                rs(dn, c, -1).start()

    def out_copy(c):
        rows = pl.ds(pl.multiple_of(c * CHUNK, CHUNK), CHUNK)
        return pltpu.make_async_copy(outb.at[c], out.at[:, rows, :], out_sem.at[c])

    def rs_final(c):
        @pl.when(z > 0)
        def _():
            rs(z, c, 1).wait_recv()
            own[c] = own[c] + rlo[c, z].astype(jnp.float32)

        @pl.when(z < n - 1)
        def _():
            rs(z, c, -1).wait_recv()
            own[c] = own[c] + rhi[c, z].astype(jnp.float32)

        for s in range(STEPS):
            outb[c, s] = own[c, pl.ds(s * CHUNK, CHUNK), :].astype(jnp.bfloat16)
        out_copy(c).start()

    def chunk(c, carry):
        base = c * CHUNK
        ag_arrive(c, n - 1)
        for s in range(STEPS):
            square = jnp.zeros((CHUNK, 1), jnp.float32)
            for o in range(n):
                wide = xall[o, c, s].astype(jnp.float32)
                square += jnp.sum(wide * wide, axis=-1, keepdims=True)
            factor = lax.rsqrt(square * (1.0 / (n * dl)) + RMS_EPS)
            for o in range(n):
                wide = xall[o, c, s].astype(jnp.float32)
                normed[o, pl.ds(s * CHUNK, CHUNK), :] = (wide * factor * gain[o]).astype(jnp.bfloat16)

        def project(i, carry):
            cols = pl.ds(pl.multiple_of(i * 256, 256), 256)
            acc = jnp.zeros((TOK, 256), jnp.float32)
            for o in range(n):
                acc += jnp.dot(
                    normed[o], wqkv[pl.ds(o * dl, dl), cols], preferred_element_type=jnp.float32
                )
            qkv[:, cols] = acc
            return carry

        lax.fori_loop(0, width // 256, project, 0)

        if chunks > 2:
            @pl.when(c == 0)
            def _():
                for d in range(2, n - 1):
                    ag_arrive(2, d)

        @pl.when(c > 0)
        def _():
            rs_forward(c - 1)

        rows = pl.ds(pl.multiple_of(base, CHUNK), CHUNK)
        attend(
            kv_local, qkv, lambda s: cos[s, rows, :], lambda s: sin[s, rows, :],
            lambda r: lens[r], ckb, cvb, base, at, q3, k3, v3, a3,
        )

        @pl.when(c > 0)
        def _():
            rs_final(c - 1)

        def project_out(p, carry):
            terms = jnp.dot(at[...], wout[p], preferred_element_type=jnp.float32)
            parts[c, p] = terms.astype(jnp.bfloat16)

            @pl.when(p == z)
            def _():
                own[c] = terms

            return carry

        lax.fori_loop(0, n, project_out, 0)
        rs_first(c)
        return carry

    lax.fori_loop(0, chunks, chunk, 0)
    rs_forward(chunks - 1)
    rs_final(chunks - 1)

    for c in range(chunks):
        out_copy(c).wait()
        for o in range(n):
            @pl.when((o <= z) & (z < n - 1))
            def _():
                ag(o, c, 1).wait_send()

            @pl.when((o >= z) & (z > 0))
            def _():
                ag(o, c, -1).wait_send()

            @pl.when(o > z)
            def _():
                rs(o, c, 1).wait_send()

            @pl.when(o < z)
            def _():
                rs(o, c, -1).wait_send()

    for dy in range(1, ny):
        fac_y(dy).wait_send()
    for dy in range(ny):
        fac_across(dy).wait_send()


def shards(
    x, norm_gain, query_weight, key_weight, value_weight, output_weight,
    query_down, key_down, value_down, output_down,
    query_up, key_up_factor, value_up, output_up,
    cached_keys, cached_values, context_lengths,
):
    n, n_fsdp = lax.axis_size("tp"), lax.axis_size("fsdp")
    steps, nrows, dl = x.shape
    chunks = nrows // CHUNK
    ql, kl = query_weight.shape[1], key_weight.shape[1]
    d = n * dl
    kv_local = kl // HF
    sizes = (query_down.shape[0], output_down.shape[0], key_up_factor.shape[0])
    pack = jnp.concatenate([
        jnp.concatenate([query_down, key_down], 1),
        jnp.concatenate([value_down, output_up], 1),
        jnp.concatenate([query_up, output_down], 1),
        jnp.concatenate([value_up, key_up_factor], 1),
    ])
    gain = norm_gain.astype(jnp.float32).reshape(n, 1, dl)
    cos, sin = rope_tables(context_lengths)
    wo_split = dl % HF != 0
    if wo_split:
        output_weight = output_weight.reshape(ql, n, dl).transpose(1, 0, 2)
    bf, f32 = jnp.bfloat16, jnp.float32
    vm = pltpu.VMEM
    hbm = pl.BlockSpec(memory_space=pl.ANY)
    vmem = pl.BlockSpec(memory_space=pltpu.VMEM)
    smem = pl.BlockSpec(memory_space=pltpu.SMEM)
    heads = vm((CHUNK, kv_local * 8, HF), f32)
    block = vm((chunks, n, TOK, dl), bf)
    dma = pltpu.SemaphoreType.DMA
    return pl.pallas_call(
        functools.partial(layer_kernel, n, n_fsdp, chunks, sizes, wo_split),
        out_shape=jax.ShapeDtypeStruct((steps, nrows, dl), bf),
        in_specs=[smem, hbm, vmem, hbm, hbm, hbm, hbm, hbm, vmem, vmem, hbm, hbm],
        out_specs=hbm,
        scratch_shapes=[
            vm((n, chunks, STEPS, CHUNK, dl), bf),
            vm((n_fsdp,) + pack.shape, bf),
            vm((d, ql + 2 * kl), bf),
            vm((n, ql, dl), bf),
            vm(cached_keys.shape, bf),
            vm(cached_values.shape, bf),
            vm((ql + kl, HF), bf),
            vm((kl, HF), bf),
            vm((ql, HF), bf),
            vm((n, TOK, dl), bf),
            vm((TOK, ql + 2 * kl), f32),
            vm((TOK, ql), bf),
            heads, heads, heads, heads,
            block,
            vm((chunks, TOK, dl), f32),
            block, block,
            vm((chunks, STEPS, CHUNK, dl), bf),
            dma((n, chunks)), dma((n, chunks)), dma((n, chunks)),
            dma((chunks, n)), dma((chunks, n)), dma((chunks, n)), dma((chunks, n)),
            dma((n_fsdp // 2,)), dma((n_fsdp // 2,)), dma((n_fsdp,)),
            dma((chunks,)), dma((3 + n,)), dma((2,)), dma(()), dma((chunks,)),
        ],
        compiler_params=pltpu.CompilerParams(
            collective_id=0, has_side_effects=True, vmem_limit_bytes=60 * 2**20
        ),
    )(
        context_lengths, x, gain, query_weight, key_weight, value_weight, output_weight,
        pack, cos, sin, cached_keys, cached_values,
    )


def solution(mesh):
    fs = ("groups", "fsdp")
    return jax.shard_map(
        shards,
        mesh=mesh,
        in_specs=(
            P(None, fs, "tp"), P(),
            P(None, "tp"), P(None, "tp"), P(None, "tp"), P("tp", None),
            P(fs, None), P(fs, None), P(fs, None), P(fs, None),
            P(fs, None), P(fs, None), P(fs, None), P(fs, None),
            P(fs, "tp", None, None), P(fs, "tp", None, None), P(fs),
        ),
        out_specs=P(None, fs, "tp"),
        check_vma=False,
    )
```
